256 devices in a mesh: rep: 16 (over y_lo, z), fsdp: 16 (over y_hi, x, core).
Axes of the slice: x: 4, y: 4 (y_hi: 2, y_lo: 2; y = y_hi * 2 + y_lo), z: 8, core: 2. Of those that a mesh axis runs over, the one named last changes fastest.
Arguments:
- grads: bfloat16 [16, 16, 4, 128, 5120], P('rep', 'fsdp'), may hold values from -6 to 6
- momentum: float32 [16, 4, 128, 5120], P('rep', None, 'fsdp'), may hold values from -6 to 6
- params: float32 [4, 128, 5120], P(None, 'fsdp'), may hold values from -6 to 6
- band: int32 [4, 128, 80, 16], P(None, 'fsdp'), may hold values from 0 to 63, as said below
Outputs:
- new_momentum: float32 [16, 4, 128, 5120], P('rep', None, 'fsdp')
- new_params: float32 [4, 128, 5120], P(None, 'fsdp')
The draws below stay inside these ranges and needn't reach their ends.
Inputs may be any that keep to these rules, and one draw needn't show every extreme that they name: `band`: the 16 indices of one block are distinct.
All inputs are finite; a program needn't handle non-finite values.
Results may differ from the reference program's by a relative error of at most 0.0003.
Values sent between devices are 32-bit elements; how exact they have to be, the bound alone decides.
No kernel may reach another device: no remote copies, remote signals or barrier semaphores. Data moves between devices by JAX's collectives and lax.ppermute only.
A program may use at most 64 MiB of HBM per device.

```python
import jax
import jax.numpy as jnp
from jax import lax

D = 5120
SPAN = 64
BAND = 16
LAYERS = 4
ROWS = 128
NCHUNK = 80
N_REP = 16
N_FSDP = 16


def draw_band(key, part):
    key = jax.random.fold_in(key, 7)
    base = jnp.broadcast_to(jnp.arange(SPAN, dtype=jnp.int32), (LAYERS * ROWS * NCHUNK, SPAN))
    shuffled = jax.random.permutation(key, base, axis=1, independent=True)
    return shuffled[:, :BAND].reshape(LAYERS, ROWS, NCHUNK, BAND).astype(jnp.int32)


def strengthened(values, rng, source, target, blocks, factor):
    owner, partner = [(jnp.arange(values.shape[dim]) // (values.shape[dim] // blocks)).reshape([-1 if axis == dim else 1 for axis in range(values.ndim)]) for dim in (source, target)]
    chosen = jax.random.permutation(rng, blocks)[partner]
    strong = (owner == chosen) | (owner == (partner + blocks // 2) % blocks)
    return jnp.where(strong, factor * values, values)


def levels(key, dims, pieces, low, high):
    loudness = 1.0
    for position, blocks in pieces:
        draws = jax.random.uniform(jax.random.fold_in(jax.random.fold_in(key, 6), position), (blocks,), jnp.float32, low / len(pieces), high / len(pieces))
        loudness = loudness * jnp.repeat(jnp.exp(draws), dims[position] // blocks).reshape((-1,) + (1,) * (len(dims) - 1 - position))
    return loudness


def gaussian(stream_key, dims, deviation, reach, shards=(), kind=jnp.bfloat16):
    values = jax.random.normal(stream_key, dims, jnp.float32) * deviation
    if len(shards) > 0:
        values = levels(stream_key, dims, shards, -0.22, 0.18) * values
    return jnp.clip(values, min=-reach, max=reach).astype(kind)


def gaussian_with(stream_key, dims, scale, limit, shards, heavy, held_as=jnp.bfloat16):
    array = scale * jax.random.normal(stream_key, dims, jnp.float32)
    if shards:
        array = array * levels(stream_key, dims, shards, -0.22, 0.18)
    return jnp.clip(strengthened(array, jax.random.fold_in(stream_key, 3), *heavy), -limit, limit).astype(held_as)


def setup_inputs(seed: int = 0) -> dict:
    streams_of = jax.random.split(jax.random.key(seed), 5)
    grads = gaussian_with(streams_of[0], (N_REP, N_FSDP, LAYERS, ROWS, D), 1.0, 6.0, ((0, 16), (1, 16)), (1, 3, 16, 2.0))
    momentum = gaussian(streams_of[1], (N_REP, LAYERS, ROWS, D), 1.0, 6.0, ((0, 16), (2, 16)), jnp.float32)
    params = gaussian(streams_of[2], (LAYERS, ROWS, D), 1.0, 6.0, ((1, 16),), jnp.float32)
    band = draw_band(jax.random.fold_in(streams_of[4], 71), 0)
    return {"grads": grads, "momentum": momentum, "params": params, "band": band}


def dct_table():
    index = jnp.arange(SPAN, dtype=jnp.float32)
    angle = jnp.pi * (2.0 * index[None, :] + 1.0) * index[:, None] / (2.0 * SPAN)
    scales = jnp.where(index == 0.0, jnp.sqrt(1.0 / SPAN), jnp.sqrt(2.0 / SPAN)).astype(jnp.float32)
    return (scales[:, None] * jnp.cos(angle)).astype(jnp.float32)

def band_inverse(values, select, table):
    dense = jnp.einsum('licj,licjk->lick', values, select, precision=lax.Precision.HIGHEST)
    blocks = jnp.einsum('lick,kn->licn', dense, table, precision=lax.Precision.HIGHEST)
    return blocks.reshape(LAYERS, ROWS, D)

def reference(grads, momentum, params, band):
    table = dct_table()
    select = (band[..., None] == jnp.arange(SPAN, dtype=jnp.int32)).astype(jnp.float32)

    def add_part(index, total):
        return total + grads[:, index].astype(jnp.float32)
    summed = lax.fori_loop(0, N_FSDP, add_part, jnp.zeros((N_REP, LAYERS, ROWS, D), jnp.float32))

    def one_replica(pair):
        grad_sum, moment = pair
        pre = 0.9 * moment + grad_sum
        blocks = pre.reshape(LAYERS, ROWS, NCHUNK, SPAN)
        coeffs = jnp.einsum('licn,kn->lick', blocks, table, precision=lax.Precision.HIGHEST)
        values = jnp.take_along_axis(coeffs, band, axis=-1)
        kept = pre - band_inverse(values, select, table)
        return (kept, values)
    new_momentum, values = lax.map(one_replica, (summed, momentum))
    mean_values = lax.optimization_barrier(jnp.sum(values, axis=0)) / N_REP
    update = band_inverse(mean_values, select, table)
    return (new_momentum, params - 0.5 * update)
```

```python
import jax
import jax.numpy as jnp
import numpy as np
from jax import lax
from jax.experimental import pallas as pl
from jax.experimental.pallas import tpu as pltpu
from jax.sharding import PartitionSpec as P

SPAN = 64
BAND = 16
LANES = 128
EXACT = lax.Precision.HIGHEST
CHUNKS = ((0, 2), (2, 2))
ORDERS = ((1, 2, 0), (2, 0, 1), (0, 1, 2))


def table128():
    k = np.arange(SPAN, dtype=np.float64)[:, None]
    n = np.arange(SPAN, dtype=np.float64)[None, :]
    scale = np.where(k == 0, np.sqrt(1.0 / SPAN), np.sqrt(2.0 / SPAN))
    table = (scale * np.cos(np.pi * (2 * n + 1) * k / (2 * SPAN))).astype(np.float32)
    wide = np.zeros((LANES, LANES), np.float32)
    wide[:SPAN, :SPAN] = table
    wide[SPAN:, SPAN:] = table
    return jnp.asarray(wide)


def fsdp_index(y, x, c):
    return (y * 4 + x) * 2 + c


def fsdp_pairs(step):
    return [
        (fsdp_index(y, x, c), fsdp_index(*step(y, x, c)))
        for y in range(2)
        for x in range(4)
        for c in range(2)
    ]


CORE = fsdp_pairs(lambda y, x, c: (y, x, 1 - c))
HALVES = (
    fsdp_pairs(lambda y, x, c: (1 - y, x, c)),
    fsdp_pairs(lambda y, x, c: (y, x ^ 1, c)),
    fsdp_pairs(lambda y, x, c: (y, 3 - x, c)),
)


def rep_pairs(mask):
    return [(i, i ^ mask) for i in range(16)]


def split_cores(grads, chips, core, first, count):
    width = grads.shape[2]

    def kernel(chips_ref, core_ref, grads_ref, other_ref, own_ref):
        both = grads_ref[...].astype(jnp.float32)
        low, high = both[:, :8], both[:, 8:]
        is_low = core_ref[0] == 0
        own_ref[0] = jnp.where(is_low, low, high)
        other_ref[0] = jnp.where(is_low, high, low)

    out = jax.ShapeDtypeStruct((8, count, 8, width), jnp.float32)
    spec = pl.BlockSpec((1, count, 8, width), lambda i, chips, core: (i, 0, 0, 0))
    return pl.pallas_call(
        kernel,
        grid_spec=pltpu.PrefetchScalarGridSpec(
            num_scalar_prefetch=2,
            grid=(8,),
            in_specs=[
                pl.BlockSpec(
                    (count, 16, width), lambda i, chips, core: (first // count, chips[i], 0)
                )
            ],
            out_specs=[spec, spec],
        ),
        out_shape=[out, out],
        compiler_params=pltpu.CompilerParams(vmem_limit_bytes=24 * 2**20),
        name="split_cores",
    )(chips, core, grads)


def padded(count):
    return -(-count // LANES) * LANES


def to_blocks(rows):
    high, wide = rows.shape
    tiles = [rows[:, t * LANES : (t + 1) * LANES] for t in range(wide // LANES)]
    total = high * len(tiles)
    if padded(total) > total:
        tiles.append(jnp.zeros((padded(total) - total, LANES), rows.dtype))
    return jnp.concatenate(tiles, axis=0)


def forward(keeps, recvs, momentum, band, table, first, count):
    rows = 8 * count
    width = momentum.shape[2]
    blocks = band.shape[1]
    parts = len(keeps)

    def kernel(*refs):
        keep_refs, recv_refs = refs[:parts], refs[parts : 2 * parts]
        mom_ref, band_ref, table_ref, values_ref, dense_ref, pre_ref = refs[2 * parts :]
        at = 0
        for k_ref, r_ref in zip(keep_refs, recv_refs):
            wide = k_ref.shape[2]
            part = 0.9 * mom_ref[first : first + count, :, at : at + wide] + (
                k_ref[...] + r_ref[...]
            )
            pre_ref[:, at : at + wide] = part.reshape(rows, wide)
            at += wide
        cut = to_blocks(pre_ref[...])
        coeffs = lax.dot_general(
            table_ref[...],
            cut,
            (((1,), (1,)), ((), ())),
            precision=EXACT,
            preferred_element_type=jnp.float32,
        )
        index = lax.broadcasted_iota(jnp.int32, (SPAN, LANES), 0)
        for tile in range(blocks // LANES):
            lanes = slice(tile * LANES, (tile + 1) * LANES)
            for h in range(2):
                block = coeffs[h * SPAN : (h + 1) * SPAN, lanes]
                kept = jnp.zeros((SPAN, LANES), jnp.float32)
                picked = []
                for j in range(BAND):
                    hit = index == band_ref[h * BAND + j : h * BAND + j + 1, lanes]
                    one = jnp.where(hit, block, 0.0)
                    kept = kept + one
                    picked.append(jnp.sum(one, axis=0, keepdims=True))
                dense_ref[h * SPAN : (h + 1) * SPAN, lanes] = kept
                values_ref[h * BAND : (h + 1) * BAND, lanes] = jnp.concatenate(picked, axis=0)

    shapes = [
        jax.ShapeDtypeStruct((2 * BAND, blocks), jnp.float32),
        jax.ShapeDtypeStruct((LANES, blocks), jnp.float32),
        jax.ShapeDtypeStruct((rows, width), jnp.float32),
    ]
    return pl.pallas_call(
        kernel,
        out_shape=shapes,
        compiler_params=pltpu.CompilerParams(vmem_limit_bytes=24 * 2**20),
        name="forward_dct",
    )(*keeps, *recvs, momentum, band, table)


def inverse(dense, table):
    return lax.dot_general(
        dense,
        table,
        (((0,), (0,)), ((), ())),
        precision=EXACT,
        preferred_element_type=jnp.float32,
    )


def residual(pre, dense, table):
    rows, width = pre.shape

    def kernel(pre_ref, dense_ref, table_ref, out_ref):
        blocks = inverse(dense_ref[...], table_ref[...])
        for t in range(width // LANES):
            lanes = slice(t * LANES, (t + 1) * LANES)
            out_ref[:, lanes] = pre_ref[:, lanes] - blocks[t * rows : (t + 1) * rows]

    return pl.pallas_call(
        kernel,
        out_shape=jax.ShapeDtypeStruct((rows, width), jnp.float32),
        compiler_params=pltpu.CompilerParams(vmem_limit_bytes=24 * 2**20),
        name="residual",
    )(pre, dense, table)


def step_params(params, sums, band, table, replicas, first, count):
    rows = 8 * count
    width = params.shape[2]
    blocks = band.shape[1]

    def kernel(params_ref, s0_ref, s1_ref, s2_ref, s3_ref, band_ref, table_ref, out_ref, dense):
        index = lax.broadcasted_iota(jnp.int32, (SPAN, LANES), 0)
        for tile in range(blocks // LANES):
            lanes = slice(tile * LANES, (tile + 1) * LANES)
            total = (s0_ref[:, lanes] + s1_ref[:, lanes]) + (s2_ref[:, lanes] + s3_ref[:, lanes])
            mean = total / replicas
            for h in range(2):
                spread = jnp.zeros((SPAN, LANES), jnp.float32)
                for j in range(BAND):
                    row = h * BAND + j
                    hit = index == band_ref[row : row + 1, lanes]
                    spread = jnp.where(hit, mean[row : row + 1], spread)
                dense[h * SPAN : (h + 1) * SPAN, lanes] = spread
        update = inverse(dense[...], table_ref[...])
        for t in range(width // LANES):
            lanes = slice(t * LANES, (t + 1) * LANES)
            old = params_ref[first : first + count, :, lanes].reshape(rows, LANES)
            new = old - 0.5 * update[t * rows : (t + 1) * rows]
            out_ref[:, :, lanes] = new.reshape(count, 8, LANES)

    return pl.pallas_call(
        kernel,
        out_shape=jax.ShapeDtypeStruct((count, 8, width), jnp.float32),
        scratch_shapes=[pltpu.VMEM((LANES, blocks), jnp.float32)],
        compiler_params=pltpu.CompilerParams(vmem_limit_bytes=24 * 2**20),
        name="step_params",
    )(params, *sums, band, table)


def band_rows(band, first, count):
    part = band[first : first + count].reshape(count, 8, -1, 2, BAND)
    part = part.transpose(3, 4, 2, 0, 1).reshape(2 * BAND, -1)
    total = part.shape[1]
    return jnp.pad(part, ((0, 0), (0, padded(total) - total)), constant_values=SPAN)


def halve(piece, order):
    left = [0, 1, 2]
    for step, dim in enumerate(order):
        axis = left.index(dim)
        left.remove(dim)
        keep = lax.index_in_dim(piece, 0, axis, keepdims=False)
        send = lax.index_in_dim(piece, 1, axis, keepdims=False)
        recv = lax.ppermute(send, "fsdp", HALVES[dim])
        if step == 2:
            return keep, recv
        piece = keep + recv


def shards(grads, momentum, params, band):
    table = table128()
    grads = grads[0, 0]
    moment = momentum[0]
    width = grads.shape[2]
    replicas = lax.axis_size("rep")
    me = lax.axis_index("fsdp").astype(jnp.int32)
    core = (me % 2).reshape(1)
    x, y = (me // 2) % 4, me // 8
    chips = jnp.stack(
        [
            (y ^ dy) * 4 + column
            for dy in range(2)
            for column in (x, 3 - x, x ^ 1, x ^ 2)
        ]
    )
    tiles = width // LANES
    cuts = [0, (tiles + 2) // 3 * LANES, ((tiles + 2) // 3 + (tiles + 1) // 3) * LANES, width]
    kept, updated = [], []
    for first, count in CHUNKS:
        other, own = split_cores(grads, chips, core, first, count)
        got = lax.ppermute(other, "fsdp", CORE)
        bands = band_rows(band, first, count)
        keeps, recvs = [], []
        for third, order in enumerate(ORDERS):
            cols = slice(cuts[third], cuts[third + 1])
            piece = own[..., cols] + got[..., cols]
            keep, recv = halve(piece.reshape(2, 2, 2, *piece.shape[1:]), order)
            keeps.append(keep)
            recvs.append(recv)
        values, dense, pre = forward(keeps, recvs, moment, bands, table, first, count)
        near = [lax.ppermute(values, "rep", rep_pairs(m)) for m in (1, 2, 3)]
        four = (values + near[0]) + (near[1] + near[2])
        far = [lax.ppermute(four, "rep", rep_pairs(m)) for m in (4, 8, 12)]
        kept.append(residual(pre, dense, table).reshape(count, 8, width))
        updated.append(
            step_params(params, [four] + far, bands, table, replicas, first, count)
        )
    return jnp.concatenate(kept)[None], jnp.concatenate(updated)


def solution(mesh):
    placed = (
        P("rep", "fsdp", None, None, None),
        P("rep", None, "fsdp", None),
        P(None, "fsdp", None),
        P(None, "fsdp", None, None),
    )
    return jax.shard_map(
        shards,
        mesh=mesh,
        in_specs=placed,
        out_specs=(P("rep", None, "fsdp", None), P(None, "fsdp", None)),
        check_vma=False,
    )
```

```python
import jax
import jax.numpy as jnp
import numpy as np
from jax import lax
from jax.experimental import pallas as pl
from jax.experimental.pallas import tpu as pltpu
from jax.sharding import PartitionSpec as P

SPAN = 64
BAND = 16
LANES = 128
VMEM_LIMIT = 12 * 2**20
EXACT = lax.Precision.HIGHEST
CHUNKS = ((0, 2), (2, 2))
ORDERS = ((1, 2, 0), (2, 0, 1), (0, 1, 2))


def table128():
    k = np.arange(SPAN, dtype=np.float64)[:, None]
    n = np.arange(SPAN, dtype=np.float64)[None, :]
    scale = np.where(k == 0, np.sqrt(1.0 / SPAN), np.sqrt(2.0 / SPAN))
    table = (scale * np.cos(np.pi * (2 * n + 1) * k / (2 * SPAN))).astype(np.float32)
    wide = np.zeros((LANES, LANES), np.float32)
    wide[:SPAN, :SPAN] = table
    wide[SPAN:, SPAN:] = table
    return jnp.asarray(wide)


def fsdp_index(y, x, c):
    return (y * 4 + x) * 2 + c


def fsdp_pairs(step):
    return [
        (fsdp_index(y, x, c), fsdp_index(*step(y, x, c)))
        for y in range(2)
        for x in range(4)
        for c in range(2)
    ]


CORE = fsdp_pairs(lambda y, x, c: (y, x, 1 - c))
HALVES = (
    fsdp_pairs(lambda y, x, c: (1 - y, x, c)),
    fsdp_pairs(lambda y, x, c: (y, x ^ 1, c)),
    fsdp_pairs(lambda y, x, c: (y, 3 - x, c)),
)


def rep_pairs(mask):
    return [(i, i ^ mask) for i in range(16)]


def split_cores(grads, chips, core, first, count):
    width = grads.shape[2]
    chip_count = 8

    def kernel(chips_ref, core_ref, grads_ref, other_ref, own_ref, held, sems):
        def fetch(i):
            start = pl.multiple_of(chips_ref[i] * 16, 16)
            return pltpu.make_async_copy(
                grads_ref.at[pl.ds(first, count), pl.ds(start, 16)], held.at[i], sems.at[i]
            )

        for i in range(chip_count):
            fetch(i).start()
        is_low = core_ref[0] == 0
        for i in range(chip_count):
            fetch(i).wait()
            for layer in range(count):
                both = held[i, layer].astype(jnp.float32)
                own_ref[i, layer] = jnp.where(is_low, both[:8], both[8:])
                other_ref[i, layer] = jnp.where(is_low, both[8:], both[:8])

    out = jax.ShapeDtypeStruct((chip_count, count, 8, width), jnp.float32)
    smem = pl.BlockSpec(memory_space=pltpu.SMEM)
    return pl.pallas_call(
        kernel,
        in_specs=[smem, smem, pl.BlockSpec(memory_space=pltpu.HBM)],
        out_shape=[out, out],
        scratch_shapes=[
            pltpu.VMEM((chip_count, count, 16, width), grads.dtype),
            pltpu.SemaphoreType.DMA((chip_count,)),
        ],
        compiler_params=pltpu.CompilerParams(
            vmem_limit_bytes=chip_count * count * width * 8 * 12 + 2**20
        ),
        name="split_cores",
    )(chips, core, grads)


def padded(count):
    return -(-count // LANES) * LANES


def to_blocks(rows):
    high, wide = rows.shape
    tiles = [rows[:, t * LANES : (t + 1) * LANES] for t in range(wide // LANES)]
    total = high * len(tiles)
    if padded(total) > total:
        tiles.append(jnp.zeros((padded(total) - total, LANES), rows.dtype))
    return jnp.concatenate(tiles, axis=0)


def forward(keeps, recvs, momentum, band, table, first, count):
    rows = 8 * count
    width = momentum.shape[2]
    blocks = band.shape[1]
    parts = len(keeps)

    def kernel(*refs):
        keep_refs, recv_refs = refs[:parts], refs[parts : 2 * parts]
        mom_ref, band_ref, table_ref, values_ref, dense_ref, pre_ref = refs[2 * parts :]
        at = 0
        for k_ref, r_ref in zip(keep_refs, recv_refs):
            wide = k_ref.shape[2]
            part = 0.9 * mom_ref[first : first + count, :, at : at + wide] + (
                k_ref[...] + r_ref[...]
            )
            pre_ref[:, at : at + wide] = part.reshape(rows, wide)
            at += wide
        cut = to_blocks(pre_ref[...])
        coeffs = lax.dot_general(
            table_ref[...],
            cut,
            (((1,), (1,)), ((), ())),
            precision=EXACT,
            preferred_element_type=jnp.float32,
        )
        index = lax.broadcasted_iota(jnp.int32, (SPAN, LANES), 0)
        for tile in range(blocks // LANES):
            lanes = slice(tile * LANES, (tile + 1) * LANES)
            for h in range(2):
                block = coeffs[h * SPAN : (h + 1) * SPAN, lanes]
                kept = jnp.zeros((SPAN, LANES), jnp.float32)
                picked = []
                for j in range(BAND):
                    hit = index == band_ref[h * BAND + j : h * BAND + j + 1, lanes]
                    one = jnp.where(hit, block, 0.0)
                    kept = kept + one
                    picked.append(jnp.sum(one, axis=0, keepdims=True))
                dense_ref[h * SPAN : (h + 1) * SPAN, lanes] = kept
                values_ref[h * BAND : (h + 1) * BAND, lanes] = jnp.concatenate(picked, axis=0)

    shapes = [
        jax.ShapeDtypeStruct((2 * BAND, blocks), jnp.float32),
        jax.ShapeDtypeStruct((LANES, blocks), jnp.float32),
        jax.ShapeDtypeStruct((rows, width), jnp.float32),
    ]
    return pl.pallas_call(
        kernel,
        out_shape=shapes,
        compiler_params=pltpu.CompilerParams(vmem_limit_bytes=VMEM_LIMIT),
        name="forward_dct",
    )(*keeps, *recvs, momentum, band, table)


def inverse(dense, table):
    return lax.dot_general(
        dense,
        table,
        (((0,), (0,)), ((), ())),
        precision=EXACT,
        preferred_element_type=jnp.float32,
    )


def residual(pres, denses, table, layers, width):
    parts = len(CHUNKS)

    def kernel(*refs):
        pre_refs, dense_refs = refs[:parts], refs[parts : 2 * parts]
        table_ref, out_ref = refs[2 * parts :]
        for (first, count), pre_ref, dense_ref in zip(CHUNKS, pre_refs, dense_refs):
            rows = 8 * count
            blocks = inverse(dense_ref[...], table_ref[...])
            for t in range(width // LANES):
                lanes = slice(t * LANES, (t + 1) * LANES)
                new = pre_ref[:, lanes] - blocks[t * rows : (t + 1) * rows]
                out_ref[first : first + count, :, lanes] = new.reshape(count, 8, LANES)

    return pl.pallas_call(
        kernel,
        out_shape=jax.ShapeDtypeStruct((layers, 8, width), jnp.float32),
        compiler_params=pltpu.CompilerParams(vmem_limit_bytes=VMEM_LIMIT),
        name="residual",
    )(*pres, *denses, table)


def step_params(params, sums, band, table, before, replicas, first, count):
    width = params.shape[2]
    rows = 8 * count
    blocks = band.shape[1]

    def kernel(params_ref, s0_ref, s1_ref, s2_ref, s3_ref, band_ref, table_ref, *rest):
        out_ref, dense = rest[-2:]
        if before is not None:
            out_ref[:first] = rest[0][...]
        index = lax.broadcasted_iota(jnp.int32, (SPAN, LANES), 0)
        for tile in range(blocks // LANES):
            lanes = slice(tile * LANES, (tile + 1) * LANES)
            total = (s0_ref[:, lanes] + s1_ref[:, lanes]) + (s2_ref[:, lanes] + s3_ref[:, lanes])
            mean = total / replicas
            for h in range(2):
                spread = jnp.zeros((SPAN, LANES), jnp.float32)
                for j in range(BAND):
                    row = h * BAND + j
                    hit = index == band_ref[row : row + 1, lanes]
                    spread = jnp.where(hit, mean[row : row + 1], spread)
                dense[h * SPAN : (h + 1) * SPAN, lanes] = spread
        update = inverse(dense[...], table_ref[...])
        for t in range(width // LANES):
            lanes = slice(t * LANES, (t + 1) * LANES)
            old = params_ref[first : first + count, :, lanes].reshape(rows, LANES)
            new = old - 0.5 * update[t * rows : (t + 1) * rows]
            out_ref[first : first + count, :, lanes] = new.reshape(count, 8, LANES)

    extra = [] if before is None else [before]
    return pl.pallas_call(
        kernel,
        out_shape=jax.ShapeDtypeStruct((first + count, 8, width), jnp.float32),
        scratch_shapes=[pltpu.VMEM((LANES, blocks), jnp.float32)],
        compiler_params=pltpu.CompilerParams(vmem_limit_bytes=VMEM_LIMIT),
        name="step_params",
    )(params, *sums, band, table, *extra)


def band_rows(band):
    layers, _, _, spans = band.shape
    tiles = spans // 2

    def kernel(band_ref, *outs):
        for (first, count), out_ref in zip(CHUNKS, outs):
            rows = 8 * count
            blocks = out_ref.shape[1]
            index = band_ref[first : first + count].reshape(rows * BAND, spans)
            index = index.astype(jnp.float32).astype(jnp.bfloat16)
            lane = lax.broadcasted_iota(jnp.int32, (spans, blocks), 1)
            chunk = lax.broadcasted_iota(jnp.int32, (spans, blocks), 0)
            row_of = lax.broadcasted_iota(jnp.int32, (BAND, blocks), 1) % rows
            for h in range(2):
                place = (chunk == 2 * (lane // rows) + h).astype(jnp.float32).astype(jnp.bfloat16)
                spread = jnp.dot(index, place, preferred_element_type=jnp.float32)
                found = jnp.zeros((BAND, blocks), jnp.float32)
                for r in range(rows):
                    found = jnp.where(row_of == r, spread[r * BAND : (r + 1) * BAND], found)
                out_ref[h * BAND : (h + 1) * BAND] = found.astype(jnp.int32)

    return pl.pallas_call(
        kernel,
        out_shape=[
            jax.ShapeDtypeStruct((2 * BAND, padded(8 * count * tiles)), jnp.int32)
            for _, count in CHUNKS
        ],
        compiler_params=pltpu.CompilerParams(vmem_limit_bytes=VMEM_LIMIT),
        name="band_rows",
    )(band)


def halve(pieces, step):
    keeps, recvs = [], []
    for piece, order in zip(pieces, ORDERS):
        dim = order[step]
        axis = sorted(order[step:]).index(dim)
        keeps.append(lax.index_in_dim(piece, 0, axis, keepdims=False))
        send = lax.index_in_dim(piece, 1, axis, keepdims=False)
        recvs.append(lax.ppermute(send, "fsdp", HALVES[dim]))
    return keeps, list(lax.optimization_barrier(tuple(recvs)))


def ring_pairs(even, odd):
    return [
        (y * 8 + z, y * 8 + (z + (odd if z % 2 else even)) % 8) for y in range(2) for z in range(8)
    ]


OPPOSITE, BESIDE, BEYOND = ring_pairs(-3, 3), ring_pairs(-1, 1), ring_pairs(-2, 2)


def shards(grads, momentum, params, band):
    table = table128()
    grads = grads[0, 0]
    moment = momentum[0]
    layers, _, width = params.shape
    replicas = lax.axis_size("rep")
    me = lax.axis_index("fsdp").astype(jnp.int32)
    core = (me % 2).reshape(1)
    x, y = (me // 2) % 4, me // 8
    chips = jnp.stack(
        [(y ^ dy) * 4 + column for dy in range(2) for column in (x, 3 - x, x ^ 1, x ^ 2)]
    )
    tiles = width // LANES
    cuts = [0, (tiles + 2) // 3 * LANES, ((tiles + 2) // 3 + (tiles + 1) // 3) * LANES, width]
    bands = band_rows(band.transpose(0, 1, 3, 2))
    source = pltpu.with_memory_space_constraint(grads, pltpu.HBM)
    pieces = []
    for first, count in CHUNKS:
        other, own = split_cores(source, chips, core, first, count)
        got = lax.ppermute(other, "fsdp", CORE)
        both = [
            own[..., low:high] + got[..., low:high] for low, high in zip(cuts[:-1], cuts[1:])
        ]
        pieces.append([p.reshape(2, 2, 2, *p.shape[1:]) for p in both])
    for step in range(3):
        halved = [halve(p, step) for p in pieces]
        if step < 2:
            pieces = [[k + r for k, r in zip(*h)] for h in halved]
    forwards = []
    for (first, count), (keeps, recvs), bands_here in zip(CHUNKS, halved, bands):
        forwards.append(forward(keeps, recvs, moment, bands_here, table, first, count))
    updated = None
    for (first, count), (values, _, _), bands_here in zip(CHUNKS, forwards, bands):
        near = [lax.ppermute(values, "rep", rep_pairs(m)) for m in (1, 8, 9)]
        four = (values + near[0]) + (near[1] + near[2])
        far = [lax.ppermute(four, "rep", p) for p in (OPPOSITE, BESIDE, BEYOND)]
        updated = step_params(
            params, [four] + far, bands_here, table, updated, replicas, first, count
        )
    kept = residual(
        [f[2] for f in forwards], [f[1] for f in forwards], table, layers, width
    )
    return kept[None], updated


def solution(mesh):
    placed = (
        P("rep", "fsdp", None, None, None),
        P("rep", None, "fsdp", None),
        P(None, "fsdp", None),
        P(None, "fsdp", None, None),
    )
    return jax.shard_map(
        shards,
        mesh=mesh,
        in_specs=placed,
        out_specs=(P("rep", None, "fsdp", None), P(None, "fsdp", None)),
        check_vma=False,
    )
```

```python
import jax
import jax.numpy as jnp
import numpy as np
from jax import lax
from jax.experimental import pallas as pl
from jax.experimental.pallas import tpu as pltpu
from jax.sharding import PartitionSpec as P

SPAN = 64
BAND = 16
LANES = 128
VMEM_LIMIT = 10 * 2**20
EXACT = lax.Precision.HIGHEST
CHUNKS = ((0, 2), (2, 2))
PIECES = (
    ((10, (0, 1, 2)), (10, (1, 2, 0)), (20, (2, 0, 1))),
    ((20, (0, 1, 2)), (20, (1, 2, 0))),
)


def table128():
    k = np.arange(SPAN, dtype=np.float64)[:, None]
    n = np.arange(SPAN, dtype=np.float64)[None, :]
    scale = np.where(k == 0, np.sqrt(1.0 / SPAN), np.sqrt(2.0 / SPAN))
    table = (scale * np.cos(np.pi * (2 * n + 1) * k / (2 * SPAN))).astype(np.float32)
    wide = np.zeros((LANES, LANES), np.float32)
    wide[:SPAN, :SPAN] = table
    wide[SPAN:, SPAN:] = table
    return jnp.asarray(wide)


def fsdp_index(y, x, c):
    return (y * 4 + x) * 2 + c


def fsdp_pairs(step):
    return [
        (fsdp_index(y, x, c), fsdp_index(*step(y, x, c)))
        for y in range(2)
        for x in range(4)
        for c in range(2)
    ]


CORE = fsdp_pairs(lambda y, x, c: (y, x, 1 - c))
HALVES = (
    fsdp_pairs(lambda y, x, c: (1 - y, x, c)),
    fsdp_pairs(lambda y, x, c: (y, x ^ 1, c)),
    fsdp_pairs(lambda y, x, c: (y, 3 - x, c)),
)


def rep_pairs(mask):
    return [(i, i ^ mask) for i in range(16)]


def split_cores(grads, first, count):
    width = grads.shape[2]
    cube = [(dy, a, b) for dy in range(2) for a in range(2) for b in range(2)]

    def kernel(grads_ref, other_ref, own_ref, held, sems):
        me = lax.axis_index("fsdp")
        core, x, y = me % 2, (me // 2) % 4, me // 8
        across = {(0, 0): x, (0, 1): 3 - x, (1, 0): x + 1 - 2 * (x % 2), (1, 1): (x + 2) % 4}

        def fetch(side, i):
            dy, a, b = cube[i]
            chip = (1 - y if dy else y) * 4 + across[a, b]
            start = (chip * 2 + (core if side else 1 - core)) * 8
            return pltpu.make_async_copy(
                grads_ref.at[pl.ds(first, count), pl.ds(pl.multiple_of(start, 8), 8)],
                held.at[side, i],
                sems.at[side, i],
            )

        for side in range(2):
            for i in range(8):
                fetch(side, i).start()
        for side, out_ref in enumerate((other_ref, own_ref)):
            for i in range(8):
                fetch(side, i).wait()
                for layer in range(count):
                    out_ref[i, layer] = held[side, i, layer].astype(jnp.float32)

    out = jax.ShapeDtypeStruct((8, count, 8, width), jnp.float32)
    return pl.pallas_call(
        kernel,
        in_specs=[pl.BlockSpec(memory_space=pltpu.HBM)],
        out_shape=[out, out],
        scratch_shapes=[
            pltpu.VMEM((2, 8, count, 8, width), grads.dtype),
            pltpu.SemaphoreType.DMA((2, 8)),
        ],
        compiler_params=pltpu.CompilerParams(vmem_limit_bytes=VMEM_LIMIT),
        name="split_cores",
    )(grads)


def padded(count):
    return -(-count // LANES) * LANES


def to_blocks(rows):
    high, wide = rows.shape
    tiles = [rows[:, t * LANES : (t + 1) * LANES] for t in range(wide // LANES)]
    total = high * len(tiles)
    if padded(total) > total:
        tiles.append(jnp.zeros((padded(total) - total, LANES), rows.dtype))
    return jnp.concatenate(tiles, axis=0)


def forward(keeps, recvs, momentum, band, table, first, count):
    rows = 8 * count
    width = momentum.shape[2]
    blocks = band.shape[1]
    parts = len(keeps)

    def kernel(*refs):
        keep_refs, recv_refs = refs[:parts], refs[parts : 2 * parts]
        mom_ref, band_ref, table_ref, values_ref, dense_ref, pre_ref = refs[2 * parts :]
        at = 0
        for k_ref, r_ref in zip(keep_refs, recv_refs):
            wide = k_ref.shape[2]
            part = 0.9 * mom_ref[first : first + count, :, at : at + wide] + (
                k_ref[...] + r_ref[...]
            )
            pre_ref[:, at : at + wide] = part.reshape(rows, wide)
            at += wide
        cut = to_blocks(pre_ref[...])
        coeffs = lax.dot_general(
            table_ref[...],
            cut,
            (((1,), (1,)), ((), ())),
            precision=EXACT,
            preferred_element_type=jnp.float32,
        )
        index = lax.broadcasted_iota(jnp.int32, (SPAN, LANES), 0)
        for tile in range(blocks // LANES):
            lanes = slice(tile * LANES, (tile + 1) * LANES)
            for h in range(2):
                block = coeffs[h * SPAN : (h + 1) * SPAN, lanes]
                kept = jnp.zeros((SPAN, LANES), jnp.float32)
                picked = []
                for j in range(BAND):
                    hit = index == band_ref[h * BAND + j : h * BAND + j + 1, lanes]
                    one = jnp.where(hit, block, 0.0)
                    kept = kept + one
                    picked.append(jnp.sum(one, axis=0, keepdims=True))
                dense_ref[h * SPAN : (h + 1) * SPAN, lanes] = kept
                values_ref[h * BAND : (h + 1) * BAND, lanes] = jnp.concatenate(picked, axis=0)

    shapes = [
        jax.ShapeDtypeStruct((2 * BAND, blocks), jnp.float32),
        jax.ShapeDtypeStruct((LANES, blocks), jnp.float32),
        jax.ShapeDtypeStruct((rows, width), jnp.float32),
    ]
    return pl.pallas_call(
        kernel,
        out_shape=shapes,
        compiler_params=pltpu.CompilerParams(vmem_limit_bytes=VMEM_LIMIT),
        name="forward_dct",
    )(*keeps, *recvs, momentum, band, table)


def inverse(dense, table):
    return lax.dot_general(
        dense,
        table,
        (((0,), (0,)), ((), ())),
        precision=EXACT,
        preferred_element_type=jnp.float32,
    )


def residual(pres, denses, table, layers, width):
    parts = len(CHUNKS)

    def kernel(*refs):
        pre_refs, dense_refs = refs[:parts], refs[parts : 2 * parts]
        table_ref, out_ref = refs[2 * parts :]
        for (first, count), pre_ref, dense_ref in zip(CHUNKS, pre_refs, dense_refs):
            rows = 8 * count
            blocks = inverse(dense_ref[...], table_ref[...])
            for t in range(width // LANES):
                lanes = slice(t * LANES, (t + 1) * LANES)
                new = pre_ref[:, lanes] - blocks[t * rows : (t + 1) * rows]
                out_ref[first : first + count, :, lanes] = new.reshape(count, 8, LANES)

    return pl.pallas_call(
        kernel,
        out_shape=jax.ShapeDtypeStruct((layers, 8, width), jnp.float32),
        compiler_params=pltpu.CompilerParams(vmem_limit_bytes=VMEM_LIMIT),
        name="residual",
    )(*pres, *denses, table)


def step_params(params, sums, band, table, before, replicas, first, count):
    layers, _, width = params.shape
    rows = 8 * count
    blocks = band.shape[1]
    pieces = 5
    wide = width // pieces

    def kernel(params_ref, s0_ref, s1_ref, s2_ref, s3_ref, band_ref, table_ref, *rest):
        out_ref, dense, held, sems = rest[-4:]
        index = lax.broadcasted_iota(jnp.int32, (SPAN, LANES), 0)
        for tile in range(blocks // LANES):
            lanes = slice(tile * LANES, (tile + 1) * LANES)
            total = (s0_ref[:, lanes] + s1_ref[:, lanes]) + (s2_ref[:, lanes] + s3_ref[:, lanes])
            mean = total / replicas
            for h in range(2):
                spread = jnp.zeros((SPAN, LANES), jnp.float32)
                for j in range(BAND):
                    row = h * BAND + j
                    hit = index == band_ref[row : row + 1, lanes]
                    spread = jnp.where(hit, mean[row : row + 1], spread)
                dense[h * SPAN : (h + 1) * SPAN, lanes] = spread
        update = inverse(dense[...], table_ref[...])
        copies = []
        for piece in range(pieces):
            for t in range(piece * wide // LANES, (piece + 1) * wide // LANES):
                lanes = slice(t * LANES, (t + 1) * LANES)
                old = params_ref[first : first + count, :, lanes].reshape(rows, LANES)
                new = old - 0.5 * update[t * rows : (t + 1) * rows]
                held[:, :, lanes] = new.reshape(count, 8, LANES)
            lanes = pl.ds(piece * wide, wide)
            copies.append(
                pltpu.make_async_copy(
                    held.at[:, :, lanes],
                    out_ref.at[pl.ds(first, count), :, lanes],
                    sems.at[piece],
                )
            )
            copies[-1].start()
        for copy in copies:
            copy.wait()

    extra = [] if before is None else [before]
    vmem = pl.BlockSpec(memory_space=pltpu.VMEM)
    anywhere = pl.BlockSpec(memory_space=pl.ANY)
    return pl.pallas_call(
        kernel,
        in_specs=[vmem] * 7 + [anywhere] * len(extra),
        out_specs=anywhere,
        out_shape=jax.ShapeDtypeStruct((layers, 8, width), jnp.float32),
        scratch_shapes=[
            pltpu.VMEM((LANES, blocks), jnp.float32),
            pltpu.VMEM((count, 8, width), jnp.float32),
            pltpu.SemaphoreType.DMA((pieces,)),
        ],
        input_output_aliases={7: 0} if extra else {},
        compiler_params=pltpu.CompilerParams(vmem_limit_bytes=VMEM_LIMIT),
        name="step_params",
    )(params, *sums, band, table, *extra)


def band_rows(band):
    layers, _, _, spans = band.shape
    tiles = spans // 2

    def kernel(band_ref, *outs):
        for (first, count), out_ref in zip(CHUNKS, outs):
            rows = 8 * count
            blocks = out_ref.shape[1]
            index = band_ref[first : first + count].reshape(rows * BAND, spans)
            index = index.astype(jnp.float32).astype(jnp.bfloat16)
            lane = lax.broadcasted_iota(jnp.int32, (spans, blocks), 1)
            chunk = lax.broadcasted_iota(jnp.int32, (spans, blocks), 0)
            row_of = lax.broadcasted_iota(jnp.int32, (BAND, blocks), 1) % rows
            for h in range(2):
                place = (chunk == 2 * (lane // rows) + h).astype(jnp.float32).astype(jnp.bfloat16)
                spread = jnp.dot(index, place, preferred_element_type=jnp.float32)
                found = jnp.zeros((BAND, blocks), jnp.float32)
                for r in range(rows):
                    found = jnp.where(row_of == r, spread[r * BAND : (r + 1) * BAND], found)
                out_ref[h * BAND : (h + 1) * BAND] = found.astype(jnp.int32)

    return pl.pallas_call(
        kernel,
        out_shape=[
            jax.ShapeDtypeStruct((2 * BAND, padded(8 * count * tiles)), jnp.int32)
            for _, count in CHUNKS
        ],
        compiler_params=pltpu.CompilerParams(vmem_limit_bytes=VMEM_LIMIT),
        name="band_rows",
    )(band)


def halve(pieces, orders, step):
    keeps, recvs = [], []
    for piece, order in zip(pieces, orders):
        axis = sorted(order[step:]).index(order[step])
        keep, send = [lax.index_in_dim(piece, i, axis, keepdims=False) for i in range(2)]
        keeps.append(keep)
        recvs.append(lax.ppermute(send, "fsdp", HALVES[order[step]]))
    return keeps, list(lax.optimization_barrier(tuple(recvs)))


def ring_pairs(even, odd):
    return [
        (y * 8 + z, y * 8 + (z + (odd if z % 2 else even)) % 8) for y in range(2) for z in range(8)
    ]


OPPOSITE, BESIDE, BEYOND = ring_pairs(-3, 3), ring_pairs(-1, 1), ring_pairs(-2, 2)


def shards(grads, momentum, params, band):
    table = table128()
    grads = grads[0, 0]
    moment = momentum[0]
    layers, _, width = params.shape
    replicas = lax.axis_size("rep")
    bands = band_rows(band.transpose(0, 1, 3, 2))
    source = pltpu.with_memory_space_constraint(grads, pltpu.HBM)
    pieces, orders = [], []
    for (first, count), parts in zip(CHUNKS, PIECES):
        other, own = split_cores(source, first, count)
        got = lax.ppermute(other, "fsdp", CORE)
        at = 0
        both = []
        for tiles, _ in parts:
            lanes = slice(at, at + tiles * LANES)
            part = own[..., lanes] + got[..., lanes]
            both.append(part.reshape(2, 2, 2, *part.shape[1:]))
            at += tiles * LANES
        pieces.append(both)
        orders.append([order for _, order in parts])
    for step in range(3):
        halved = [halve(p, o, step) for p, o in zip(pieces, orders)]
        if step < 2:
            pieces = [[k + r for k, r in zip(*h)] for h in halved]
    forwards = []
    for (first, count), (keeps, recvs), bands_here in zip(CHUNKS, halved, bands):
        forwards.append(forward(keeps, recvs, moment, bands_here, table, first, count))
    updated = None
    for (first, count), (values, _, _), bands_here in zip(CHUNKS, forwards, bands):
        near = [lax.ppermute(values, "rep", rep_pairs(m)) for m in (1, 8, 9)]
        four = (values + near[0]) + (near[1] + near[2])
        far = [lax.ppermute(four, "rep", p) for p in (OPPOSITE, BESIDE, BEYOND)]
        updated = step_params(
            params, [four] + far, bands_here, table, updated, replicas, first, count
        )
    kept = residual(
        [f[2] for f in forwards], [f[1] for f in forwards], table, layers, width
    )
    return kept[None], updated


def solution(mesh):
    placed = (
        P("rep", "fsdp", None, None, None),
        P("rep", None, "fsdp", None),
        P(None, "fsdp", None),
        P(None, "fsdp", None, None),
    )
    return jax.shard_map(
        shards,
        mesh=mesh,
        in_specs=placed,
        out_specs=(P("rep", None, "fsdp", None), P(None, "fsdp", None)),
        check_vma=False,
    )
```

```python
import jax
import jax.numpy as jnp
import numpy as np
from jax import lax
from jax.experimental import pallas as pl
from jax.experimental.pallas import tpu as pltpu
from jax.sharding import PartitionSpec as P

SPAN = 64
BAND = 16
LANES = 128
VMEM_LIMIT = 10 * 2**20
EXACT = lax.Precision.HIGHEST
CHUNKS = ((0, 2), (2, 2))
PIECES = (
    ((10, (0, 1, 2)), (10, (1, 2, 0)), (20, (2, 0, 1))),
    ((20, (0, 1, 2)), (20, (1, 2, 0))),
)


def table128():
    k = np.arange(SPAN, dtype=np.float64)[:, None]
    n = np.arange(SPAN, dtype=np.float64)[None, :]
    scale = np.where(k == 0, np.sqrt(1.0 / SPAN), np.sqrt(2.0 / SPAN))
    table = (scale * np.cos(np.pi * (2 * n + 1) * k / (2 * SPAN))).astype(np.float32)
    wide = np.zeros((LANES, LANES), np.float32)
    wide[:SPAN, :SPAN] = table
    wide[SPAN:, SPAN:] = table
    return jnp.asarray(wide)


def fsdp_index(y, x, c):
    return (y * 4 + x) * 2 + c


def fsdp_pairs(step):
    return [
        (fsdp_index(y, x, c), fsdp_index(*step(y, x, c)))
        for y in range(2)
        for x in range(4)
        for c in range(2)
    ]


CORE = fsdp_pairs(lambda y, x, c: (y, x, 1 - c))
HALVES = (
    fsdp_pairs(lambda y, x, c: (1 - y, x, c)),
    fsdp_pairs(lambda y, x, c: (y, x ^ 1, c)),
    fsdp_pairs(lambda y, x, c: (y, 3 - x, c)),
)


def rep_pairs(mask):
    return [(i, i ^ mask) for i in range(16)]


def split_cores(grads, first, count):
    width = grads.shape[2]
    cube = [(dy, a, b) for dy in range(2) for a in range(2) for b in range(2)]

    def kernel(grads_ref, other_ref, own_ref, held, sems):
        me = lax.axis_index("fsdp")
        core, x, y = me % 2, (me // 2) % 4, me // 8
        across = {(0, 0): x, (0, 1): 3 - x, (1, 0): x + 1 - 2 * (x % 2), (1, 1): (x + 2) % 4}

        def fetch(i):
            dy, a, b = cube[i]
            start = ((1 - y if dy else y) * 4 + across[a, b]) * 16
            return pltpu.make_async_copy(
                grads_ref.at[pl.ds(first, count), pl.ds(pl.multiple_of(start, 16), 16)],
                held.at[i],
                sems.at[i],
            )

        for i in range(8):
            fetch(i).start()
        is_low = core == 0
        for i in range(8):
            fetch(i).wait()
            for layer in range(count):
                both = held[i, layer].astype(jnp.float32)
                own_ref[i, layer] = jnp.where(is_low, both[:8], both[8:])
                other_ref[i, layer] = jnp.where(is_low, both[8:], both[:8])

    out = jax.ShapeDtypeStruct((8, count, 8, width), jnp.float32)
    return pl.pallas_call(
        kernel,
        in_specs=[pl.BlockSpec(memory_space=pltpu.HBM)],
        out_shape=[out, out],
        scratch_shapes=[
            pltpu.VMEM((8, count, 16, width), grads.dtype),
            pltpu.SemaphoreType.DMA((8,)),
        ],
        compiler_params=pltpu.CompilerParams(vmem_limit_bytes=VMEM_LIMIT),
        name="split_cores",
    )(grads)


def padded(count):
    return -(-count // LANES) * LANES


def to_blocks(rows):
    high, wide = rows.shape
    tiles = [rows[:, t * LANES : (t + 1) * LANES] for t in range(wide // LANES)]
    total = high * len(tiles)
    if padded(total) > total:
        tiles.append(jnp.zeros((padded(total) - total, LANES), rows.dtype))
    return jnp.concatenate(tiles, axis=0)


def forward(keeps, recvs, momentum, band, table, first, count):
    rows = 8 * count
    width = momentum.shape[2]
    blocks = band.shape[1]
    parts = len(keeps)

    def kernel(*refs):
        keep_refs, recv_refs = refs[:parts], refs[parts : 2 * parts]
        mom_ref, band_ref, table_ref, values_ref, dense_ref, pre_ref = refs[2 * parts :]
        at = 0
        for k_ref, r_ref in zip(keep_refs, recv_refs):
            wide = k_ref.shape[2]
            part = 0.9 * mom_ref[first : first + count, :, at : at + wide] + (
                k_ref[...] + r_ref[...]
            )
            pre_ref[:, at : at + wide] = part.reshape(rows, wide)
            at += wide
        cut = to_blocks(pre_ref[...])
        coeffs = lax.dot_general(
            table_ref[...],
            cut,
            (((1,), (1,)), ((), ())),
            precision=EXACT,
            preferred_element_type=jnp.float32,
        )
        index = lax.broadcasted_iota(jnp.int32, (SPAN, LANES), 0)
        for tile in range(blocks // LANES):
            lanes = slice(tile * LANES, (tile + 1) * LANES)
            for h in range(2):
                block = coeffs[h * SPAN : (h + 1) * SPAN, lanes]
                kept = jnp.zeros((SPAN, LANES), jnp.float32)
                picked = []
                for j in range(BAND):
                    hit = index == band_ref[h * BAND + j : h * BAND + j + 1, lanes]
                    one = jnp.where(hit, block, 0.0)
                    kept = kept + one
                    picked.append(jnp.sum(one, axis=0, keepdims=True))
                dense_ref[h * SPAN : (h + 1) * SPAN, lanes] = kept
                values_ref[h * BAND : (h + 1) * BAND, lanes] = jnp.concatenate(picked, axis=0)

    shapes = [
        jax.ShapeDtypeStruct((2 * BAND, blocks), jnp.float32),
        jax.ShapeDtypeStruct((LANES, blocks), jnp.float32),
        jax.ShapeDtypeStruct((rows, width), jnp.float32),
    ]
    return pl.pallas_call(
        kernel,
        out_shape=shapes,
        compiler_params=pltpu.CompilerParams(vmem_limit_bytes=VMEM_LIMIT),
        name="forward_dct",
    )(*keeps, *recvs, momentum, band, table)


def inverse(dense, table):
    return lax.dot_general(
        dense,
        table,
        (((0,), (0,)), ((), ())),
        precision=EXACT,
        preferred_element_type=jnp.float32,
    )


def residual(pres, denses, table, layers, width):
    parts = len(CHUNKS)

    def kernel(*refs):
        pre_refs, dense_refs = refs[:parts], refs[parts : 2 * parts]
        table_ref, out_ref = refs[2 * parts :]
        for (first, count), pre_ref, dense_ref in zip(CHUNKS, pre_refs, dense_refs):
            rows = 8 * count
            blocks = inverse(dense_ref[...], table_ref[...])
            for t in range(width // LANES):
                lanes = slice(t * LANES, (t + 1) * LANES)
                new = pre_ref[:, lanes] - blocks[t * rows : (t + 1) * rows]
                out_ref[first : first + count, :, lanes] = new.reshape(count, 8, LANES)

    return pl.pallas_call(
        kernel,
        out_shape=jax.ShapeDtypeStruct((layers, 8, width), jnp.float32),
        compiler_params=pltpu.CompilerParams(vmem_limit_bytes=VMEM_LIMIT),
        name="residual",
    )(*pres, *denses, table)


def step_params(params, sums, band, table, before, replicas, first, count):
    layers, _, width = params.shape
    rows = 8 * count
    blocks = band.shape[1]
    pieces = 5
    wide = width // pieces

    def kernel(params_ref, s0_ref, s1_ref, s2_ref, s3_ref, band_ref, table_ref, *rest):
        out_ref, dense, held, sems = rest[-4:]
        index = lax.broadcasted_iota(jnp.int32, (SPAN, LANES), 0)
        for tile in range(blocks // LANES):
            lanes = slice(tile * LANES, (tile + 1) * LANES)
            total = (s0_ref[:, lanes] + s1_ref[:, lanes]) + (s2_ref[:, lanes] + s3_ref[:, lanes])
            mean = total / replicas
            for h in range(2):
                spread = jnp.zeros((SPAN, LANES), jnp.float32)
                for j in range(BAND):
                    row = h * BAND + j
                    hit = index == band_ref[row : row + 1, lanes]
                    spread = jnp.where(hit, mean[row : row + 1], spread)
                dense[h * SPAN : (h + 1) * SPAN, lanes] = spread
        update = inverse(dense[...], table_ref[...])
        copies = []
        for piece in range(pieces):
            for t in range(piece * wide // LANES, (piece + 1) * wide // LANES):
                lanes = slice(t * LANES, (t + 1) * LANES)
                old = params_ref[first : first + count, :, lanes].reshape(rows, LANES)
                new = old - 0.5 * update[t * rows : (t + 1) * rows]
                held[:, :, lanes] = new.reshape(count, 8, LANES)
            lanes = pl.ds(piece * wide, wide)
            copies.append(
                pltpu.make_async_copy(
                    held.at[:, :, lanes],
                    out_ref.at[pl.ds(first, count), :, lanes],
                    sems.at[piece],
                )
            )
            copies[-1].start()
        for copy in copies:
            copy.wait()

    extra = [] if before is None else [before]
    vmem = pl.BlockSpec(memory_space=pltpu.VMEM)
    anywhere = pl.BlockSpec(memory_space=pl.ANY)
    return pl.pallas_call(
        kernel,
        in_specs=[vmem] * 7 + [anywhere] * len(extra),
        out_specs=anywhere,
        out_shape=jax.ShapeDtypeStruct((layers, 8, width), jnp.float32),
        scratch_shapes=[
            pltpu.VMEM((LANES, blocks), jnp.float32),
            pltpu.VMEM((count, 8, width), jnp.float32),
            pltpu.SemaphoreType.DMA((pieces,)),
        ],
        input_output_aliases={7: 0} if extra else {},
        compiler_params=pltpu.CompilerParams(vmem_limit_bytes=VMEM_LIMIT),
        name="step_params",
    )(params, *sums, band, table, *extra)


def band_rows(band):
    layers, _, _, spans = band.shape
    tiles = spans // 2

    def kernel(band_ref, *outs):
        for (first, count), out_ref in zip(CHUNKS, outs):
            rows = 8 * count
            blocks = out_ref.shape[1]
            index = band_ref[first : first + count].reshape(rows * BAND, spans)
            index = index.astype(jnp.float32).astype(jnp.bfloat16)
            lane = lax.broadcasted_iota(jnp.int32, (spans, blocks), 1)
            chunk = lax.broadcasted_iota(jnp.int32, (spans, blocks), 0)
            row_of = lax.broadcasted_iota(jnp.int32, (BAND, blocks), 1) % rows
            for h in range(2):
                place = (chunk == 2 * (lane // rows) + h).astype(jnp.float32).astype(jnp.bfloat16)
                spread = jnp.dot(index, place, preferred_element_type=jnp.float32)
                found = jnp.zeros((BAND, blocks), jnp.float32)
                for r in range(rows):
                    found = jnp.where(row_of == r, spread[r * BAND : (r + 1) * BAND], found)
                out_ref[h * BAND : (h + 1) * BAND] = found.astype(jnp.int32)

    return pl.pallas_call(
        kernel,
        out_shape=[
            jax.ShapeDtypeStruct((2 * BAND, padded(8 * count * tiles)), jnp.int32)
            for _, count in CHUNKS
        ],
        compiler_params=pltpu.CompilerParams(vmem_limit_bytes=VMEM_LIMIT),
        name="band_rows",
    )(band)


def halve(pieces, orders, step):
    keeps, recvs = [], []
    for piece, order in zip(pieces, orders):
        axis = sorted(order[step:]).index(order[step])
        keep, send = [lax.index_in_dim(piece, i, axis, keepdims=False) for i in range(2)]
        keeps.append(keep)
        recvs.append(lax.ppermute(send, "fsdp", HALVES[order[step]]))
    return keeps, list(lax.optimization_barrier(tuple(recvs)))


def ring_pairs(even, odd):
    return [
        (y * 8 + z, y * 8 + (z + (odd if z % 2 else even)) % 8) for y in range(2) for z in range(8)
    ]


OPPOSITE, BESIDE, BEYOND = ring_pairs(-3, 3), ring_pairs(-1, 1), ring_pairs(-2, 2)


def shards(grads, momentum, params, band):
    table = table128()
    grads = grads[0, 0]
    moment = momentum[0]
    layers, _, width = params.shape
    replicas = lax.axis_size("rep")
    bands = band_rows(band.transpose(0, 1, 3, 2))
    source = pltpu.with_memory_space_constraint(grads, pltpu.HBM)
    pieces, orders = [], []
    for (first, count), parts in zip(CHUNKS, PIECES):
        other, own = split_cores(source, first, count)
        got = lax.ppermute(other, "fsdp", CORE)
        at = 0
        both = []
        for tiles, _ in parts:
            lanes = slice(at, at + tiles * LANES)
            part = own[..., lanes] + got[..., lanes]
            both.append(part.reshape(2, 2, 2, *part.shape[1:]))
            at += tiles * LANES
        pieces.append(both)
        orders.append([order for _, order in parts])
    for step in range(3):
        halved = [halve(p, o, step) for p, o in zip(pieces, orders)]
        if step < 2:
            pieces = [[k + r for k, r in zip(*h)] for h in halved]
    forwards = []
    for (first, count), (keeps, recvs), bands_here in zip(CHUNKS, halved, bands):
        forwards.append(forward(keeps, recvs, moment, bands_here, table, first, count))
    updated = None
    for (first, count), (values, _, _), bands_here in zip(CHUNKS, forwards, bands):
        near = [lax.ppermute(values, "rep", rep_pairs(m)) for m in (1, 8, 9)]
        four = (values + near[0]) + (near[1] + near[2])
        far = [lax.ppermute(four, "rep", p) for p in (OPPOSITE, BESIDE, BEYOND)]
        updated = step_params(
            params, [four] + far, bands_here, table, updated, replicas, first, count
        )
    kept = residual(
        [f[2] for f in forwards], [f[1] for f in forwards], table, layers, width
    )
    return kept[None], updated


def solution(mesh):
    placed = (
        P("rep", "fsdp", None, None, None),
        P("rep", None, "fsdp", None),
        P(None, "fsdp", None),
        P(None, "fsdp", None, None),
    )
    return jax.shard_map(
        shards,
        mesh=mesh,
        in_specs=placed,
        out_specs=(P("rep", None, "fsdp", None), P(None, "fsdp", None)),
        check_vma=False,
    )
```
